32 devices in a mesh: group: 2 (over x), node: 8 (over z, y), local: 2 (over core).
Axes of the slice: x: 2, y: 2, z: 4, core: 2. Of those that a mesh axis runs over, the one named last changes fastest.
Arguments:
- tokens: bfloat16 [2048, 3584], P(('group', 'node', 'local')), parts along dimension 0, may hold values from -6 to 6
- routes: int32 [2048, 8], P(('group', 'node', 'local')), parts along dimension 0, may hold values from 0 to 15, all different within a row; in each aligned block of 64 rows (0 to 63, 64 to 127, ...) at most 40 rows name the same one
- gate_values: bfloat16 [2048, 8], P(('group', 'node', 'local')), parts along dimension 0, may hold values from 0.049804688 to 0.29882812
- gate_weight: bfloat16 [16, 3584, 1024], P(('node', 'local')), may hold values from -0.09375 to 0.09375
- up_weight: bfloat16 [16, 3584, 1024], P(('node', 'local')), may hold values from -0.09375 to 0.09375
- down_weight: bfloat16 [16, 1024, 3584], P(('node', 'local')), may hold values from -0.1875 to 0.1875
Outputs:
- mixed: bfloat16 [2048, 3584], P(('group', 'node', 'local')), parts along dimension 0
The draws below stay inside these ranges and needn't reach their ends.
There are 2 independent parts, one for each index of `group`. The reference program is written for one: setup_inputs(seed, part) draws one part's arguments, and reference() takes and returns one part's arrays. A program takes and returns all parts, laid end to end along the dimension named above; an argument that names none is the same for every part. Nothing has to cross between parts.
Inputs may be any that keep to these rules, and one draw needn't show every extreme that they name: `routes`: A token's 8 expert copies are distinct; of the 64 tokens of one device at most 40 name one expert copy, a bound that some block reaches of them.
All inputs are finite; a program needn't handle non-finite values.
Results may differ from the reference program's by a relative error of at most 0.0058.
Values may be sent and summed in bfloat16 or wider, within the bound.
No kernel may reach another device: no remote copies, remote signals or barrier semaphores. Data moves between devices by JAX's collectives and lax.ppermute only.
A program may use at most 128 MiB of HBM per device.

```python
import math
import jax
import jax.numpy as jnp
import numpy as np
from jax import lax

D = 3584
FF = 1024
TOPK = 8
TOK_DEV = 64
TOKENS = 1024
SLOTS = 16
CAP = 40
N_NODE = 8
N_LOCAL = 2


def steps_of(rng, extent, split, low, high):
    def one(axis_at, shards_of):
        heights = jax.random.uniform(jax.random.fold_in(jax.random.fold_in(rng, 6), axis_at), (shards_of,), jnp.float32, low / len(split), high / len(split))
        return jnp.repeat(jnp.exp(heights), extent[axis_at] // shards_of).reshape((-1,) + (1,) * (len(extent) - axis_at - 1))

    loudness = one(*split[0])
    for cut in split[1:]:
        loudness = loudness * one(*cut)
    return loudness


def deal_out(stream_key, own, number, rows, amount, top, most, skew):
    order = jax.random.permutation(stream_key, amount)
    heavy_load, common = shares(amount, rows * top, most, skew, True), shares(amount, rows * top, most, skew, False)
    places = jnp.arange(amount)

    def named(lengths, turn):
        used = int((lengths > 0).sum())
        fixed = max(1, used // 4)
        shifted = fixed + (places - fixed + turn * (used - fixed)) % max(1, amount - fixed)
        return jnp.zeros((amount,), jnp.int32).at[order[jnp.where(places < fixed, places, shifted)]].set(jnp.asarray(lengths, jnp.int32))

    lengths = jnp.where(number % 4 == 0, named(heavy_load, number // 4), named(common, number - number // 4 - 1))
    mixed = jax.random.permutation(jax.random.fold_in(own, 3), amount)
    source_of, taker = mixed[0:amount // 2 * 2:2], mixed[1:amount // 2 * 2:2]
    slack = jnp.minimum(lengths[source_of] - 1, most - lengths[taker]) // 2
    slack = jnp.where((source_of == order[0]) | (taker == order[0]) | (lengths[taker] == 0), 0, jnp.maximum(slack, 0))
    shifted = jax.random.randint(jax.random.fold_in(own, 4), (amount // 2,), 0, 1 << 20) % (slack + 1)
    lengths = lengths.at[source_of].add(-shifted).at[taker].add(shifted)
    labels = jnp.searchsorted(jnp.cumsum(lengths), jnp.arange(rows * top), side="right").astype(jnp.int32)
    grid = labels.reshape(top, rows).T
    grid = grid[jax.random.permutation(jax.random.fold_in(own, 1), rows)]
    turn = jax.random.randint(jax.random.fold_in(own, 2), (rows, 1), 0, top)
    return jnp.take_along_axis(grid, (jnp.arange(top)[None, :] + turn) % top, axis=1)


def shares(amount, total, most, skew, full):
    weights = [(1 << 20) // math.isqrt(grade ** skew) + 1 for grade in range(1, amount + 1)]
    largest = most if full else min(most, max(-(-total // amount), total * weights[0] // sum(weights)))
    least = 1 if total - largest >= amount - 1 else 0
    counts, surplus = [largest] + [least] * (amount - 1), total - largest - least * (amount - 1)
    while surplus > 0:
        movable = [i for i in range(1, amount) if counts[i] < largest] or [i for i in range(1, amount) if counts[i] < most]
        pool, budget = sum([weights[i] for i in movable]), surplus
        for i in movable:
            more = min(most - counts[i], max(1, budget * weights[i] // pool), surplus)
            counts[i] = counts[i] + more
            surplus = surplus - more
    return np.array(counts)


def normal_values(own_key, extent, spread, reach, shards=(), kind=jnp.bfloat16):
    drawn = jax.random.normal(own_key, extent, jnp.float32) * spread
    if len(shards) > 0:
        drawn = steps_of(own_key, extent, shards, -0.22, 0.18) * drawn
    return jnp.clip(drawn, min=-reach, max=reach).astype(kind)


def setup_inputs(seed: int = 0, part: int = 0) -> dict:
    arg_keys = jax.random.split(jax.random.key(seed), 7)
    own_keys = jax.random.split(jax.random.fold_in(arg_keys[6], part), 7)
    tokens = normal_values(own_keys[0], (TOKENS, D), 1.0, 6.0, ((0, 16),))
    routes_keys = jax.random.split(jax.random.fold_in(own_keys[1], 1), TOKENS // TOK_DEV)
    routes_turns = jax.random.permutation(jax.random.fold_in(own_keys[1], 3), TOKENS // TOK_DEV)
    routes = jax.vmap(lambda own, number: deal_out(jax.random.fold_in(own_keys[1], 2), own, number, TOK_DEV, SLOTS, TOPK, CAP, 2))(routes_keys, routes_turns).reshape((TOKENS, TOPK))
    gate_values = jnp.clip(0.049804688 + 0.24902344 * jax.random.uniform(own_keys[2], (TOKENS, TOPK), jnp.float32) ** steps_of(own_keys[2], (TOKENS, TOPK), ((0, 16),), -0.2, 0.2), 0.049804688, 0.29882812).astype(jnp.bfloat16)
    gate_weight = normal_values(arg_keys[3], (SLOTS, D, FF), D ** -0.5, 0.09375, ((0, 16),))
    up_weight = normal_values(arg_keys[4], (SLOTS, D, FF), D ** -0.5, 0.09375, ((0, 16),))
    down_weight = normal_values(arg_keys[5], (SLOTS, FF, D), FF ** -0.5, 0.1875, ((0, 16),))
    return {"tokens": tokens, "routes": routes, "gate_values": gate_values, "gate_weight": gate_weight, "up_weight": up_weight, "down_weight": down_weight}


def expert(inputs, w_gate, w_up, w_down):
    gate_part = jnp.dot(inputs, w_gate, preferred_element_type=jnp.float32)
    upper_part = jnp.dot(inputs, w_up, preferred_element_type=jnp.float32)
    hidden = (jax.nn.silu(gate_part) * upper_part).astype(jnp.bfloat16)
    return jnp.dot(hidden, w_down, preferred_element_type=jnp.float32).astype(jnp.bfloat16)


def placement_of(route_ids, slot_count, capacity):
    flat_ids = route_ids.reshape(-1).astype(jnp.int32)
    one_hot = (flat_ids[:, None] == jnp.arange(slot_count, dtype=jnp.int32)[None, :]).astype(jnp.int32)
    before = jnp.cumsum(one_hot, axis=0, dtype=jnp.int32) - one_hot
    position = jnp.sum(before * one_hot, axis=1, dtype=jnp.int32)
    return (flat_ids * capacity + position).astype(jnp.int32)


def reference(tokens, routes, gate_values, gate_weight, up_weight, down_weight):
    ep_devices = N_NODE * N_LOCAL
    source_routes = routes.reshape(ep_devices, TOK_DEV * TOPK)
    target = jax.vmap(lambda route_ids: placement_of(route_ids, SLOTS, CAP))(source_routes)
    copies = jnp.repeat(tokens, TOPK, axis=0).reshape(ep_devices, TOK_DEV * TOPK, D)
    buffers = jax.vmap(lambda spots, values: jnp.zeros((SLOTS * CAP, D), jnp.bfloat16).at[spots].set(values))(target, copies)
    per_slot = buffers.reshape(ep_devices, SLOTS, CAP, D).transpose(1, 0, 2, 3).reshape(SLOTS, ep_devices * CAP, D)
    results = lax.map(lambda packed: expert(packed[0], packed[1], packed[2], packed[3]), (per_slot, gate_weight, up_weight, down_weight))
    returned = results.reshape(SLOTS, ep_devices, CAP, D).transpose(1, 0, 2, 3).reshape(ep_devices, SLOTS * CAP, D)
    picked = jax.vmap(lambda block, spots: block[spots])(returned, target)
    picked = picked.astype(jnp.float32).reshape(TOKENS, TOPK, D)
    mixed = jnp.sum(picked * gate_values.astype(jnp.float32)[:, :, None], axis=1)
    return mixed.astype(jnp.bfloat16)
```

```python
import functools

import jax
import jax.numpy as jnp
from jax import lax
from jax.experimental import pallas as pl
from jax.experimental.pallas import tpu as pltpu
from jax.sharding import PartitionSpec as P

CHUNKS = 2
LANES = 128
HIDDEN_TILE = 256
OUT_TILE = 512


def expert_kernel(count, model_width, hidden_steps, *refs):
    pieces = refs[:count]
    pick_ref, gate_ref, up_ref, down_ref, own_ref, other_ref = refs[count : count + 6]
    x_ref, h_ref, g_ref, sems = refs[count + 6 :]
    step = pl.program_id(0)
    rows = pieces[0].shape[0]

    @pl.when(step == 0)
    def _():
        copies = [
            pltpu.make_async_copy(piece, x_ref.at[pl.ds(n * rows, rows)], sems.at[n])
            for n, piece in enumerate(pieces)
        ]
        for copy in copies:
            copy.start()
        for copy in copies:
            copy.wait()
        chosen = x_ref[:, model_width:].astype(jnp.float32) * pick_ref[...]
        g_ref[...] = jnp.broadcast_to(jnp.sum(chosen, axis=1, keepdims=True), g_ref.shape)

    @pl.when(step < hidden_steps)
    def _():
        x = x_ref[:, :model_width]
        gate = jnp.dot(x, gate_ref[...], preferred_element_type=jnp.float32)
        up = jnp.dot(x, up_ref[...], preferred_element_type=jnp.float32)
        width = gate_ref.shape[1]
        h_ref[:, pl.ds(pl.multiple_of(step * width, width), width)] = (
            gate / (1.0 + jnp.exp(-gate)) * up
        ).astype(jnp.bfloat16)

    @pl.when(step >= hidden_steps)
    def _():
        out = jnp.dot(h_ref[...], down_ref[...], preferred_element_type=jnp.float32)
        out = (out * g_ref[:, :1]).astype(jnp.bfloat16)
        half = own_ref.shape[0]
        own_ref[...] = out[:half]
        other_ref[...] = out[half:]


def expert(own, other, pick, w_gate, w_up, w_down):
    pieces = own + other
    count = len(pieces)
    rows = count * pieces[0].shape[0]
    model_width, hidden_width = w_gate.shape
    hidden_steps = hidden_width // HIDDEN_TILE
    out_steps = model_width // OUT_TILE
    hidden_block = pl.BlockSpec(
        (model_width, HIDDEN_TILE), lambda i: (0, jnp.minimum(i, hidden_steps - 1))
    )
    out_block = pl.BlockSpec(
        (rows // 2, OUT_TILE), lambda i: (0, jnp.maximum(i - hidden_steps, 0))
    )
    result = jax.ShapeDtypeStruct((rows // 2, model_width), jnp.bfloat16)
    return pl.pallas_call(
        functools.partial(expert_kernel, count, model_width, hidden_steps),
        grid=(hidden_steps + out_steps,),
        in_specs=[pl.BlockSpec(memory_space=pl.ANY)] * count
        + [
            pl.BlockSpec((1, LANES), lambda i: (0, 0)),
            hidden_block,
            hidden_block,
            pl.BlockSpec(
                (hidden_width, OUT_TILE), lambda i: (0, jnp.maximum(i - hidden_steps, 0))
            ),
        ],
        out_specs=[out_block, out_block],
        out_shape=[result, result],
        scratch_shapes=[
            pltpu.VMEM((rows, pieces[0].shape[1]), jnp.bfloat16),
            pltpu.VMEM((rows, hidden_width), jnp.bfloat16),
            pltpu.VMEM((rows, LANES), jnp.float32),
            pltpu.SemaphoreType.DMA((count,)),
        ],
        compiler_params=pltpu.CompilerParams(
            dimension_semantics=("arbitrary",), vmem_limit_bytes=24 * 1024 * 1024
        ),
        cost_estimate=pl.CostEstimate(
            flops=6 * rows * model_width * hidden_width,
            bytes_accessed=6 * model_width * hidden_width,
            transcendentals=rows * hidden_width,
        ),
        name="expert",
    )(*pieces, pick, w_gate, w_up, w_down)


def ring_of(count):
    order = list(range(0, count, 2)) + list(range(count - 1, 0, -2))
    return [(order[i], order[(i + 1) % count]) for i in range(count)]


def shards(tokens, routes, gate_values, gate_weight, up_weight, down_weight):
    tok_count, model_width = tokens.shape
    nodes = lax.axis_size("node")
    locals_ = lax.axis_size("local")
    slots = nodes * locals_
    half = nodes // 2
    core = lax.axis_index("local")
    me = lax.axis_index("node") * locals_ + core
    ring = ring_of(nodes)
    back = [(b, a) for a, b in ring]
    split = [(locals_ * a, locals_ * b) for a, b in ring] + [
        (locals_ * a + 1, locals_ * b + 1) for a, b in back
    ]
    both = ("node", "local")

    def onward(v):
        return lax.ppermute(v, "node", ring)

    def backward(v):
        return lax.ppermute(v, "node", back)

    def swap(v):
        return lax.ppermute(v, "local", [(0, 1), (1, 0)])

    wide = jnp.arange(LANES, dtype=jnp.int32)
    dense = jnp.sum(
        jnp.where(
            routes[:, :, None] == wide[None, None, :],
            gate_values.astype(jnp.float32)[:, :, None],
            0.0,
        ),
        axis=1,
    ).astype(jnp.bfloat16)
    pick = (wide == me).astype(jnp.float32)[None, :]
    packed = jnp.concatenate([tokens, dense], axis=1)
    size = tok_count // CHUNKS
    weights = (gate_weight[0], up_weight[0], down_weight[0])

    gathered = []
    for chunk in range(CHUNKS):
        mine = packed[chunk * size : (chunk + 1) * size]
        ahead, behind = {0: mine}, {0: mine}
        for d in range(1, half):
            ahead[d] = onward(ahead[d - 1])
            behind[d] = backward(behind[d - 1])
        far = lax.ppermute(jnp.where(core == 0, ahead[half - 1], behind[half - 1]), both, split)
        order = [("far", far), ("mine", mine)]
        for d in range(half - 1, 0, -1):
            order += [(("a", d), ahead[d]), (("b", d), behind[d])]
        gathered.append(order)

    outs = []
    for order in gathered:
        part = {}
        for start in range(0, len(order), 4):
            group = order[start : start + 4]
            own = [v for _, v in group]
            y_own, y_other = expert(own, [swap(v) for v in own], pick, *weights)
            y_swapped = swap(y_other)
            for n, (key, _) in enumerate(group):
                cut = slice(n * size, (n + 1) * size)
                part[key] = y_own[cut].astype(jnp.float32) + y_swapped[cut].astype(jnp.float32)
        narrow = jnp.bfloat16
        got = lax.ppermute(part["far"].astype(narrow), both, split).astype(jnp.float32)
        up_in = jnp.where(core == 0, got, 0.0)
        down_in = jnp.where(core == 0, 0.0, got)
        for d in range(half - 1, 0, -1):
            up_in = onward((part["b", d] + up_in).astype(narrow)).astype(jnp.float32)
            down_in = backward((part["a", d] + down_in).astype(narrow)).astype(jnp.float32)
        outs.append((part["mine"] + up_in + down_in).astype(narrow))
    return jnp.concatenate(outs, axis=0)


def solution(mesh):
    return jax.shard_map(
        shards,
        mesh=mesh,
        in_specs=(
            P(("group", "node", "local"), None),
            P(("group", "node", "local"), None),
            P(("group", "node", "local"), None),
            P(("node", "local"), None, None),
            P(("node", "local"), None, None),
            P(("node", "local"), None, None),
        ),
        out_specs=P(("group", "node", "local"), None),
        check_vma=False,
    )
```

```python
import functools

import jax
import jax.numpy as jnp
from jax import lax
from jax.experimental import pallas as pl
from jax.experimental.pallas import tpu as pltpu
from jax.sharding import PartitionSpec as P

PARTS = 2
LANES = 128
HIDDEN_TILE = 512
OUT_TILE = 896


def expert_kernel(count, loads, *refs):
    pieces, refs = refs[:count], refs[count:]
    pick_ref, *sources, own_ref, other_ref = refs[:6]
    if loads:
        *kept, h_ref, sems = refs[6:]
    else:
        kept, (h_ref,) = sources, refs[6:]
    gate_ref, up_ref, down_ref = kept
    model_width, hidden_width = gate_ref.shape
    hidden_cuts = [pl.ds(s, HIDDEN_TILE) for s in range(0, hidden_width, HIDDEN_TILE)]
    out_cuts = [pl.ds(s, OUT_TILE) for s in range(0, model_width, OUT_TILE)]
    order = [(which, cut) for cut in hidden_cuts for which in (0, 1)]
    order += [(2, cut) for cut in out_cuts]
    copies = []
    if loads:
        for n, (which, cut) in enumerate(order):
            copies.append(
                pltpu.make_async_copy(
                    sources[which].at[:, cut], kept[which].at[:, cut], sems.at[n]
                )
            )
            copies[n].start()

    def ready():
        if copies:
            copies.pop(0).wait()

    def rows(start, size):
        return jnp.concatenate([p[:, start : start + size] for p in pieces], axis=0)

    chosen = rows(model_width, LANES).astype(jnp.float32) * pick_ref[...]
    weight = jnp.sum(chosen, axis=1, keepdims=True)
    for cut in hidden_cuts:
        x = rows(0, model_width)
        ready()
        gate = jnp.dot(x, gate_ref[:, cut], preferred_element_type=jnp.float32)
        ready()
        up = jnp.dot(x, up_ref[:, cut], preferred_element_type=jnp.float32)
        h_ref[:, cut] = (gate / (1.0 + jnp.exp(-gate)) * up).astype(jnp.bfloat16)
    half = own_ref.shape[0]
    for cut in out_cuts:
        ready()
        out = jnp.dot(h_ref[...], down_ref[:, cut], preferred_element_type=jnp.float32)
        out = (out * weight).astype(jnp.bfloat16)
        own_ref[:, cut] = out[:half]
        other_ref[:, cut] = out[half:]


def expert(own, other, pick, weights, source="hbm", keep=False):
    loads = source == "hbm"
    pieces = own + other
    count = len(pieces)
    rows = count * pieces[0].shape[0]
    model_width, hidden_width = weights[0].shape
    result = jax.ShapeDtypeStruct((rows // 2, model_width), jnp.bfloat16)
    vmem = pl.BlockSpec(memory_space=pltpu.VMEM)
    held = [pltpu.VMEM(w.shape, w.dtype) for w in weights]
    scratch = [pltpu.VMEM((rows, hidden_width), jnp.bfloat16)]
    out_shape = [result, result]
    limit = 16
    if loads:
        steps = 2 * (hidden_width // HIDDEN_TILE) + model_width // OUT_TILE
        scratch.append(pltpu.SemaphoreType.DMA((steps,)))
        if keep:
            out_shape += held
        else:
            scratch = held + scratch
            limit += 22
    space = pltpu.HBM if loads else pltpu.VMEM
    weights = [pltpu.with_memory_space_constraint(w, space) for w in weights]
    return pl.pallas_call(
        functools.partial(expert_kernel, count, loads),
        in_specs=[vmem] * (count + 1)
        + [pl.BlockSpec(memory_space=pl.ANY if loads else pltpu.VMEM)] * 3,
        out_specs=[vmem] * len(out_shape),
        out_shape=out_shape,
        scratch_shapes=scratch,
        compiler_params=pltpu.CompilerParams(vmem_limit_bytes=limit * 1024 * 1024),
        cost_estimate=pl.CostEstimate(
            flops=6 * rows * model_width * hidden_width,
            bytes_accessed=6 * model_width * hidden_width if loads else 0,
            transcendentals=rows * hidden_width,
        ),
        name="expert",
    )(*pieces, pick, *weights)


def ring_of(count):
    order = list(range(0, count, 2)) + list(range(count - 1, 0, -2))
    return [(order[i], order[(i + 1) % count]) for i in range(count)]


def shards(tokens, routes, gate_values, gate_weight, up_weight, down_weight):
    tok_count, model_width = tokens.shape
    nodes = lax.axis_size("node")
    locals_ = lax.axis_size("local")
    slots = nodes * locals_
    half = nodes // 2
    core = lax.axis_index("local")
    me = lax.axis_index("node") * locals_ + core
    ring = ring_of(nodes)
    back = [(b, a) for a, b in ring]
    split = [(locals_ * a, locals_ * b) for a, b in ring] + [
        (locals_ * a + 1, locals_ * b + 1) for a, b in back
    ]
    both = ("node", "local")

    def onward(v):
        return lax.ppermute(v, "node", ring)

    def backward(v):
        return lax.ppermute(v, "node", back)

    def swap(v):
        return lax.ppermute(v, "local", [(0, 1), (1, 0)])

    wide = jnp.arange(LANES, dtype=jnp.int32)
    dense = jnp.sum(
        jnp.where(
            routes[:, :, None] == wide[None, None, :],
            gate_values.astype(jnp.float32)[:, :, None],
            0.0,
        ),
        axis=1,
    ).astype(jnp.bfloat16)
    pick = (wide == me).astype(jnp.float32)[None, :]
    packed = jnp.concatenate([tokens, dense], axis=1)
    size = tok_count // PARTS
    weights = (gate_weight[0], up_weight[0], down_weight[0])

    narrow = jnp.bfloat16

    def tie(values, *after):
        return lax.optimization_barrier((values, after))[0]

    def run(own, *how):
        y_own, y_other, *held = expert(own, [swap(v) for v in own], pick, *how)
        y_swapped = swap(y_other)

        def total(n, part):
            cut = slice((n * PARTS + part) * size, (n * PARTS + part + 1) * size)
            return y_own[cut].astype(jnp.float32) + y_swapped[cut].astype(jnp.float32)

        return total, y_own, held

    mine_sum, token, held = run([packed], weights, "hbm", True)
    ahead, behind, near = [packed], [packed], {}
    for d in range(1, half):
        ahead.append(onward(ahead[-1]))
        behind.append(backward(behind[-1]))
        ahead[d], behind[d] = tie((ahead[d], behind[d]), token)
        if d < half - 1:
            how = (held, "vmem") if d % 2 else (weights, "hbm", True)
            near[d], token, fresh = run([ahead[d], behind[d]], *how)
            held = fresh or held
    far = lax.ppermute(jnp.where(core == 0, ahead[-1], behind[-1]), both, split)
    near[half - 1], token, _ = run([ahead[-1], behind[-1]], held, "vmem")
    far_sum, _, _ = run([tie(far, token)], held, "vmem")

    sums = [far_sum(0, part).astype(narrow) for part in range(PARTS)]
    got = [lax.ppermute(v, both, split).astype(jnp.float32) for v in sums]
    up_in = [jnp.where(core == 0, v, 0.0) for v in got]
    down_in = [jnp.where(core == 0, 0.0, v) for v in got]
    before = sums[-1]
    for d in range(half - 1, 0, -1):
        for part in range(PARTS):
            up, down = tie((up_in[part], down_in[part]), before)
            up = (near[d](1, part) + up).astype(narrow)
            down = (near[d](0, part) + down).astype(narrow)
            before = up
            up_in[part] = onward(up).astype(jnp.float32)
            down_in[part] = backward(down).astype(jnp.float32)
    outs = [
        (mine_sum(0, part) + up_in[part] + down_in[part]).astype(narrow) for part in range(PARTS)
    ]
    return jnp.concatenate(outs, axis=0)


def solution(mesh):
    return jax.shard_map(
        shards,
        mesh=mesh,
        in_specs=(
            P(("group", "node", "local"), None),
            P(("group", "node", "local"), None),
            P(("group", "node", "local"), None),
            P(("node", "local"), None, None),
            P(("node", "local"), None, None),
            P(("node", "local"), None, None),
        ),
        out_specs=P(("group", "node", "local"), None),
        check_vma=False,
    )
```

```python
import functools

import jax
import jax.numpy as jnp
from jax import lax
from jax.experimental import pallas as pl
from jax.experimental.pallas import tpu as pltpu
from jax.sharding import PartitionSpec as P

PARTS = 2
LANES = 128
HIDDEN_TILE = 512
OUT_TILE = 896


def expert_kernel(count, loads, *refs):
    pieces, refs = refs[:count], refs[count:]
    pick_ref, *sources, own_ref, other_ref = refs[:6]
    if loads:
        *kept, h_ref, sems = refs[6:]
    else:
        kept, (h_ref,) = sources, refs[6:]
    gate_ref, up_ref, down_ref = kept
    model_width, hidden_width = gate_ref.shape
    hidden_cuts = [pl.ds(s, HIDDEN_TILE) for s in range(0, hidden_width, HIDDEN_TILE)]
    out_cuts = [pl.ds(s, OUT_TILE) for s in range(0, model_width, OUT_TILE)]
    order = [(which, cut) for cut in hidden_cuts for which in (0, 1)]
    order += [(2, cut) for cut in out_cuts]
    copies = []
    if loads:
        for n, (which, cut) in enumerate(order):
            copies.append(
                pltpu.make_async_copy(
                    sources[which].at[:, cut], kept[which].at[:, cut], sems.at[n]
                )
            )
            copies[n].start()

    def ready():
        if copies:
            copies.pop(0).wait()

    def rows(start, size):
        return jnp.concatenate([p[:, start : start + size] for p in pieces], axis=0)

    chosen = rows(model_width, LANES).astype(jnp.float32) * pick_ref[...]
    weight = jnp.sum(chosen, axis=1, keepdims=True)
    for cut in hidden_cuts:
        x = rows(0, model_width)
        ready()
        gate = jnp.dot(x, gate_ref[:, cut], preferred_element_type=jnp.float32)
        ready()
        up = jnp.dot(x, up_ref[:, cut], preferred_element_type=jnp.float32)
        h_ref[:, cut] = (gate / (1.0 + jnp.exp(-gate)) * up).astype(jnp.bfloat16)
    half = own_ref.shape[0]
    for cut in out_cuts:
        ready()
        out = jnp.dot(h_ref[...], down_ref[:, cut], preferred_element_type=jnp.float32)
        out = (out * weight).astype(jnp.bfloat16)
        own_ref[:, cut] = out[:half]
        other_ref[:, cut] = out[half:]


def expert(own, other, pick, weights, source="hbm", keep=False):
    loads = source == "hbm"
    pieces = own + other
    count = len(pieces)
    rows = count * pieces[0].shape[0]
    model_width, hidden_width = weights[0].shape
    result = jax.ShapeDtypeStruct((rows // 2, model_width), jnp.bfloat16)
    vmem = pl.BlockSpec(memory_space=pltpu.VMEM)
    held = [pltpu.VMEM(w.shape, w.dtype) for w in weights]
    scratch = [pltpu.VMEM((rows, hidden_width), jnp.bfloat16)]
    out_shape = [result, result]
    limit = 8
    if loads:
        steps = 2 * (hidden_width // HIDDEN_TILE) + model_width // OUT_TILE
        scratch.append(pltpu.SemaphoreType.DMA((steps,)))
        if keep:
            out_shape += held
        else:
            scratch = held + scratch
            limit += 22
    space = pltpu.HBM if loads else pltpu.VMEM
    weights = [pltpu.with_memory_space_constraint(w, space) for w in weights]
    return pl.pallas_call(
        functools.partial(expert_kernel, count, loads),
        in_specs=[vmem] * (count + 1)
        + [pl.BlockSpec(memory_space=pl.ANY if loads else pltpu.VMEM)] * 3,
        out_specs=[vmem] * len(out_shape),
        out_shape=out_shape,
        scratch_shapes=scratch,
        compiler_params=pltpu.CompilerParams(vmem_limit_bytes=limit * 1024 * 1024),
        cost_estimate=pl.CostEstimate(
            flops=6 * rows * model_width * hidden_width,
            bytes_accessed=6 * model_width * hidden_width if loads else 0,
            transcendentals=rows * hidden_width,
        ),
        name="expert",
    )(*pieces, pick, *weights)


def add_kernel(cuts, mine_ref, other_ref, *refs):
    count = len(cuts)
    for cut, in_ref, out_ref in zip(cuts, refs[:count], refs[-count:]):
        total = mine_ref[cut, :].astype(jnp.float32) + other_ref[cut, :].astype(jnp.float32)
        out_ref[...] = (total + in_ref[...].astype(jnp.float32)).astype(out_ref.dtype)


def add(cuts, mine, other, received, after):
    vmem = pl.BlockSpec(memory_space=pltpu.VMEM)
    count = len(cuts)
    return pl.pallas_call(
        functools.partial(add_kernel, cuts),
        in_specs=[vmem] * (2 + count) + [pl.BlockSpec(memory_space=pl.ANY)],
        out_specs=[vmem] * count,
        out_shape=[jax.ShapeDtypeStruct(v.shape, v.dtype) for v in received],
        compiler_params=pltpu.CompilerParams(vmem_limit_bytes=4 * 1024 * 1024),
        cost_estimate=pl.CostEstimate(
            flops=2 * count * received[0].size, bytes_accessed=0, transcendentals=0
        ),
        name="add",
    )(mine, other, *received, after)


def pack_kernel(tokens_ref, routes_ref, gates_ref, out_ref, sem):
    model_width = tokens_ref.shape[1]
    copy = pltpu.make_async_copy(tokens_ref, out_ref.at[:, pl.ds(0, model_width)], sem)
    copy.start()
    top_count, count = routes_ref.shape
    slot = lax.broadcasted_iota(jnp.int32, (LANES, count), 0)
    gates = gates_ref[...].astype(jnp.float32)
    dense = jnp.zeros((LANES, count), jnp.float32)
    for k in range(top_count):
        dense += jnp.where(routes_ref[k : k + 1, :] == slot, gates[k : k + 1, :], 0.0)
    same = lax.broadcasted_iota(jnp.int32, (count, count), 0) == lax.broadcasted_iota(
        jnp.int32, (count, count), 1
    )
    turned = lax.dot_general(
        jnp.where(same, 1.0, 0.0).astype(jnp.bfloat16),
        dense.astype(jnp.bfloat16),
        (((1,), (1,)), ((), ())),
        preferred_element_type=jnp.float32,
    )
    out_ref[:, model_width:] = turned.astype(jnp.bfloat16)
    copy.wait()


def pack(tokens, routes, gate_values):
    vmem = pl.BlockSpec(memory_space=pltpu.VMEM)
    count, model_width = tokens.shape
    return pl.pallas_call(
        pack_kernel,
        in_specs=[pl.BlockSpec(memory_space=pl.ANY), vmem, vmem],
        out_specs=vmem,
        out_shape=jax.ShapeDtypeStruct((count, model_width + LANES), jnp.bfloat16),
        scratch_shapes=[pltpu.SemaphoreType.DMA],
        compiler_params=pltpu.CompilerParams(vmem_limit_bytes=4 * 1024 * 1024),
        name="pack",
    )(*[pltpu.with_memory_space_constraint(v, pltpu.HBM) for v in (tokens, routes.T, gate_values.T)])


def finish_kernel(mine_ref, other_ref, *refs):
    *received, out_ref = refs
    size = received[0].shape[0]
    for part in range(len(received) // 2):
        cut = slice(part * size, (part + 1) * size)
        total = mine_ref[cut, :].astype(jnp.float32) + other_ref[cut, :].astype(jnp.float32)
        for ref in received[2 * part : 2 * part + 2]:
            total += ref[...].astype(jnp.float32)
        out_ref[cut, :] = total.astype(out_ref.dtype)


def finish(mine, other, received):
    vmem = pl.BlockSpec(memory_space=pltpu.VMEM)
    return pl.pallas_call(
        finish_kernel,
        in_specs=[vmem] * (2 + len(received)),
        out_specs=vmem,
        out_shape=jax.ShapeDtypeStruct(mine.shape, mine.dtype),
        compiler_params=pltpu.CompilerParams(vmem_limit_bytes=8 * 1024 * 1024),
        name="finish",
    )(mine, other, *received)


def ring_of(count):
    order = list(range(0, count, 2)) + list(range(count - 1, 0, -2))
    return [(order[i], order[(i + 1) % count]) for i in range(count)]


def shards(tokens, routes, gate_values, gate_weight, up_weight, down_weight):
    tok_count, model_width = tokens.shape
    nodes = lax.axis_size("node")
    locals_ = lax.axis_size("local")
    slots = nodes * locals_
    half = nodes // 2
    core = lax.axis_index("local")
    me = lax.axis_index("node") * locals_ + core
    ring = ring_of(nodes)
    back = [(b, a) for a, b in ring]
    split = [(locals_ * a, locals_ * b) for a, b in ring] + [
        (locals_ * a + 1, locals_ * b + 1) for a, b in back
    ]
    both = ("node", "local")

    def onward(v):
        return lax.ppermute(v, "node", ring)

    def backward(v):
        return lax.ppermute(v, "node", back)

    def swap(v):
        return lax.ppermute(v, "local", [(0, 1), (1, 0)])

    wide = jnp.arange(LANES, dtype=jnp.int32)
    pick = (wide == me).astype(jnp.float32)[None, :]
    packed = pack(tokens, routes, gate_values)
    size = tok_count // PARTS
    weights = (gate_weight[0], up_weight[0], down_weight[0])

    narrow = jnp.bfloat16

    def tie(values, *after):
        return lax.optimization_barrier((values, after))[0]

    def run(own, *how):
        y_own, y_other, *held = expert(own, [swap(v) for v in own], pick, *how)
        y_swapped = swap(y_other)

        def total(n, part):
            cut = slice(n * tok_count + part * size, n * tok_count + (part + 1) * size)
            return y_own[cut].astype(jnp.float32) + y_swapped[cut].astype(jnp.float32)

        def added(part, received, after):
            cuts = [
                slice(n * tok_count + part * size, n * tok_count + (part + 1) * size)
                for n in range(len(received))
            ]
            return add(cuts, y_own, y_swapped, received, after)

        def finished(received):
            return finish(y_own, y_swapped, received)

        return (total, added, finished), y_own, held

    def plan(d):
        return (held, "vmem") if d % 2 else (weights, "hbm", True)

    ahead, behind, near = [packed], [packed], {}
    ahead.append(onward(packed))
    behind.append(backward(packed))
    mine_sum, token, held = run([packed], *plan(0))
    for d in range(1, half):
        ahead[d], behind[d] = tie((ahead[d], behind[d]), token)
        if d < half - 1:
            ahead.append(onward(ahead[d]))
            behind.append(backward(behind[d]))
        else:
            far = lax.ppermute(jnp.where(core == 0, ahead[d], behind[d]), both, split)
        near[d], token, fresh = run([ahead[d], behind[d]], *plan(d))
        held = fresh or held
    far_sum, _, _ = run([tie(far, token)], held, "vmem")

    sums = [far_sum[0](0, part).astype(narrow) for part in range(PARTS)]
    got = [lax.ppermute(v, both, split) for v in sums]
    up_in, down_in = [None] * PARTS, [None] * PARTS
    before = sums[-1]
    for d in range(half - 1, 0, -1):
        for part in range(PARTS):
            if d == half - 1:
                up_in[part] = jnp.where(core == 0, got[part], 0)
                down_in[part] = jnp.where(core == 0, 0, got[part])
            down, up = near[d][1](part, [down_in[part], up_in[part]], before)
            before = up
            up_in[part] = onward(up)
            down_in[part] = backward(down)
    received = [v for part in range(PARTS) for v in (up_in[part], down_in[part])]
    return mine_sum[2](received)


def solution(mesh):
    return jax.shard_map(
        shards,
        mesh=mesh,
        in_specs=(
            P(("group", "node", "local"), None),
            P(("group", "node", "local"), None),
            P(("group", "node", "local"), None),
            P(("node", "local"), None, None),
            P(("node", "local"), None, None),
            P(("node", "local"), None, None),
        ),
        out_specs=P(("group", "node", "local"), None),
        check_vma=False,
    )
```

```python
import functools

import jax
import jax.numpy as jnp
from jax import lax
from jax.experimental import pallas as pl
from jax.experimental.pallas import tpu as pltpu
from jax.sharding import PartitionSpec as P

PARTS = 2
LANES = 128
HIDDEN_TILE = 512
OUT_TILE = 896


def expert_kernel(count, loads, *refs):
    pieces, refs = refs[:count], refs[count:]
    pick_ref, *sources, own_ref, other_ref = refs[:6]
    if loads:
        *kept, h_ref, sems = refs[6:]
    else:
        kept, (h_ref,) = sources, refs[6:]
    gate_ref, up_ref, down_ref = kept
    model_width, hidden_width = gate_ref.shape
    hidden_tile, out_tile = (HIDDEN_TILE, OUT_TILE) if loads else (1024, 1792)
    hidden_cuts = [pl.ds(s, hidden_tile) for s in range(0, hidden_width, hidden_tile)]
    out_cuts = [pl.ds(s, out_tile) for s in range(0, model_width, out_tile)]
    order = [(which, cut) for cut in hidden_cuts for which in (0, 1)]
    order += [(2, cut) for cut in out_cuts]
    copies = []
    if loads:
        for n, (which, cut) in enumerate(order):
            copies.append(
                pltpu.make_async_copy(
                    sources[which].at[:, cut], kept[which].at[:, cut], sems.at[n]
                )
            )
            copies[n].start()

    def ready():
        if copies:
            copies.pop(0).wait()

    def rows(start, size):
        return jnp.concatenate([p[:, start : start + size] for p in pieces], axis=0)

    chosen = rows(model_width, LANES).astype(jnp.float32) * pick_ref[...]
    weight = jnp.sum(chosen, axis=1, keepdims=True)
    for cut in hidden_cuts:
        x = rows(0, model_width)
        ready()
        gate = jnp.dot(x, gate_ref[:, cut], preferred_element_type=jnp.float32)
        ready()
        up = jnp.dot(x, up_ref[:, cut], preferred_element_type=jnp.float32)
        h_ref[:, cut] = (gate / (1.0 + jnp.exp(-gate)) * up).astype(jnp.bfloat16)
    half = own_ref.shape[0]
    for cut in out_cuts:
        ready()
        out = jnp.dot(h_ref[...], down_ref[:, cut], preferred_element_type=jnp.float32)
        out = (out * weight).astype(jnp.bfloat16)
        own_ref[:, cut] = out[:half]
        other_ref[:, cut] = out[half:]


def expert(own, other, pick, weights, source="hbm", keep=False):
    loads = source == "hbm"
    pieces = own + other
    count = len(pieces)
    rows = count * pieces[0].shape[0]
    model_width, hidden_width = weights[0].shape
    result = jax.ShapeDtypeStruct((rows // 2, model_width), jnp.bfloat16)
    vmem = pl.BlockSpec(memory_space=pltpu.VMEM)
    held = [pltpu.VMEM(w.shape, w.dtype) for w in weights]
    scratch = [pltpu.VMEM((rows, hidden_width), jnp.bfloat16)]
    out_shape = [result, result]
    limit = 12
    if loads:
        steps = 2 * (hidden_width // HIDDEN_TILE) + model_width // OUT_TILE
        scratch.append(pltpu.SemaphoreType.DMA((steps,)))
        if keep:
            out_shape += held
        else:
            scratch = held + scratch
            limit += 22
    space = pltpu.HBM if loads else pltpu.VMEM
    weights = [pltpu.with_memory_space_constraint(w, space) for w in weights]
    return pl.pallas_call(
        functools.partial(expert_kernel, count, loads),
        in_specs=[vmem] * (count + 1)
        + [pl.BlockSpec(memory_space=pl.ANY if loads else pltpu.VMEM)] * 3,
        out_specs=[vmem] * len(out_shape),
        out_shape=out_shape,
        scratch_shapes=scratch,
        compiler_params=pltpu.CompilerParams(vmem_limit_bytes=limit * 1024 * 1024),
        cost_estimate=pl.CostEstimate(
            flops=6 * rows * model_width * hidden_width,
            bytes_accessed=6 * model_width * hidden_width if loads else 0,
            transcendentals=rows * hidden_width,
        ),
        name="expert",
    )(*pieces, pick, *weights)


def add_kernel(cuts, mine_ref, other_ref, *refs):
    count = len(cuts)
    for cut, in_ref, out_ref in zip(cuts, refs[:count], refs[-count:]):
        total = mine_ref[cut, :].astype(jnp.float32) + other_ref[cut, :].astype(jnp.float32)
        out_ref[...] = (total + in_ref[...].astype(jnp.float32)).astype(out_ref.dtype)


def add(cuts, mine, other, received, after):
    vmem = pl.BlockSpec(memory_space=pltpu.VMEM)
    count = len(cuts)
    return pl.pallas_call(
        functools.partial(add_kernel, cuts),
        in_specs=[vmem] * (2 + count) + [pl.BlockSpec(memory_space=pl.ANY)],
        out_specs=[vmem] * count,
        out_shape=[jax.ShapeDtypeStruct(v.shape, v.dtype) for v in received],
        compiler_params=pltpu.CompilerParams(vmem_limit_bytes=4 * 1024 * 1024),
        cost_estimate=pl.CostEstimate(
            flops=2 * count * received[0].size, bytes_accessed=0, transcendentals=0
        ),
        name="add",
    )(mine, other, *received, after)


def pack_kernel(tokens_ref, routes_ref, gates_ref, out_ref):
    model_width = tokens_ref.shape[1]
    out_ref[:, :model_width] = tokens_ref[...]
    top_count, count = routes_ref.shape
    slot = lax.broadcasted_iota(jnp.int32, (LANES, count), 0)
    gates = gates_ref[...].astype(jnp.float32)
    dense = jnp.zeros((LANES, count), jnp.float32)
    for k in range(top_count):
        dense += jnp.where(routes_ref[k : k + 1, :] == slot, gates[k : k + 1, :], 0.0)
    same = lax.broadcasted_iota(jnp.int32, (count, count), 0) == lax.broadcasted_iota(
        jnp.int32, (count, count), 1
    )
    turned = lax.dot_general(
        jnp.where(same, 1.0, 0.0).astype(jnp.bfloat16),
        dense.astype(jnp.bfloat16),
        (((1,), (1,)), ((), ())),
        preferred_element_type=jnp.float32,
    )
    out_ref[:, model_width:] = turned.astype(jnp.bfloat16)


def pack(tokens, routes, gate_values):
    vmem = pl.BlockSpec(memory_space=pltpu.VMEM)
    count, model_width = tokens.shape
    return pl.pallas_call(
        pack_kernel,
        in_specs=[vmem, vmem, vmem],
        out_specs=vmem,
        out_shape=jax.ShapeDtypeStruct((count, model_width + LANES), jnp.bfloat16),
        compiler_params=pltpu.CompilerParams(vmem_limit_bytes=4 * 1024 * 1024),
        name="pack",
    )(*[pltpu.with_memory_space_constraint(v, pltpu.HBM) for v in (tokens, routes.T, gate_values.T)])


def finish_kernel(mine_ref, other_ref, *refs):
    *received, out_ref = refs
    size = received[0].shape[0]
    for part in range(len(received) // 2):
        cut = slice(part * size, (part + 1) * size)
        total = mine_ref[cut, :].astype(jnp.float32) + other_ref[cut, :].astype(jnp.float32)
        for ref in received[2 * part : 2 * part + 2]:
            total += ref[...].astype(jnp.float32)
        out_ref[cut, :] = total.astype(out_ref.dtype)


def finish(mine, other, received):
    vmem = pl.BlockSpec(memory_space=pltpu.VMEM)
    return pl.pallas_call(
        finish_kernel,
        in_specs=[vmem] * (2 + len(received)),
        out_specs=vmem,
        out_shape=jax.ShapeDtypeStruct(mine.shape, mine.dtype),
        compiler_params=pltpu.CompilerParams(vmem_limit_bytes=8 * 1024 * 1024),
        name="finish",
    )(mine, other, *received)


def ring_of(count):
    order = list(range(0, count, 2)) + list(range(count - 1, 0, -2))
    return [(order[i], order[(i + 1) % count]) for i in range(count)]


def shards(tokens, routes, gate_values, gate_weight, up_weight, down_weight):
    tok_count, model_width = tokens.shape
    nodes = lax.axis_size("node")
    locals_ = lax.axis_size("local")
    slots = nodes * locals_
    half = nodes // 2
    core = lax.axis_index("local")
    me = lax.axis_index("node") * locals_ + core
    ring = ring_of(nodes)
    back = [(b, a) for a, b in ring]
    split = [(locals_ * a, locals_ * b) for a, b in ring] + [
        (locals_ * a + 1, locals_ * b + 1) for a, b in back
    ]
    both = ("node", "local")

    def onward(v):
        return lax.ppermute(v, "node", ring)

    def backward(v):
        return lax.ppermute(v, "node", back)

    def swap(v):
        return lax.ppermute(v, "local", [(0, 1), (1, 0)])

    wide = jnp.arange(LANES, dtype=jnp.int32)
    pick = (wide == me).astype(jnp.float32)[None, :]
    packed = pack(tokens, routes, gate_values)
    size = tok_count // PARTS
    weights = (gate_weight[0], up_weight[0], down_weight[0])

    narrow = jnp.bfloat16

    def tie(values, *after):
        return lax.optimization_barrier((values, after))[0]

    def run(own, *how):
        y_own, y_other, *held = expert(own, [swap(v) for v in own], pick, *how)
        y_swapped = swap(y_other)

        def total(n, part):
            cut = slice(n * tok_count + part * size, n * tok_count + (part + 1) * size)
            return y_own[cut].astype(jnp.float32) + y_swapped[cut].astype(jnp.float32)

        def added(part, received, after):
            cuts = [
                slice(n * tok_count + part * size, n * tok_count + (part + 1) * size)
                for n in range(len(received))
            ]
            return add(cuts, y_own, y_swapped, received, after)

        def finished(received):
            return finish(y_own, y_swapped, received)

        return (total, added, finished), y_own, held

    def plan(d):
        return (held, "vmem") if d % 2 else (weights, "hbm", True)

    ahead, behind, near = [packed], [packed], {}
    ahead.append(onward(packed))
    behind.append(backward(packed))
    mine_sum, token, held = run([packed], *plan(0))
    for d in range(1, half):
        ahead[d], behind[d] = tie((ahead[d], behind[d]), token)
        if d < half - 1:
            ahead.append(onward(ahead[d]))
            behind.append(backward(behind[d]))
        else:
            far = lax.ppermute(jnp.where(core == 0, ahead[d], behind[d]), both, split)
        near[d], token, fresh = run([ahead[d], behind[d]], *plan(d))
        held = fresh or held
    far_sum, _, _ = run([tie(far, token)], held, "vmem")

    sums = [far_sum[0](0, part).astype(narrow) for part in range(PARTS)]
    got = [lax.ppermute(v, both, split) for v in sums]
    up_in, down_in = [None] * PARTS, [None] * PARTS
    before = sums[-1]
    for d in range(half - 1, 0, -1):
        for part in range(PARTS):
            if d == half - 1:
                up_in[part] = jnp.where(core == 0, got[part], 0)
                down_in[part] = jnp.where(core == 0, 0, got[part])
            down, up = near[d][1](part, [down_in[part], up_in[part]], before)
            before = up
            up_in[part] = onward(up)
            down_in[part] = backward(down)
    received = [v for part in range(PARTS) for v in (up_in[part], down_in[part])]
    return mine_sum[2](received)


def solution(mesh):
    return jax.shard_map(
        shards,
        mesh=mesh,
        in_specs=(
            P(("group", "node", "local"), None),
            P(("group", "node", "local"), None),
            P(("group", "node", "local"), None),
            P(("node", "local"), None, None),
            P(("node", "local"), None, None),
            P(("node", "local"), None, None),
        ),
        out_specs=P(("group", "node", "local"), None),
        check_vma=False,
    )
```
